32 devices in a mesh: lead: 8 (over z, core), grp: 4 (over y, x).
Axes of the slice: x: 2, y: 2, z: 4, core: 2. Of those that a mesh axis runs over, the one named last changes fastest.
Arguments:
- matrix_tiles: bfloat16 [64, 384, 384], P(('lead', 'grp')), may hold values from -0.0546875 to 0.0546875
- tile_slot: int32 [8, 8], P('lead'), may hold values from 0 to 7, each once within a row
- tile_cols: int32 [8, 8], P('lead'), may hold values from 0 to 2, as said below
- send_rows: int32 [8, 2, 1], replicated, may hold values from 0 to 0, as said below
- residual: float32 [3072, 128], P(('lead', 'grp')), may hold values from -6 to 6
- diag_inv: float32 [3072], P(('lead', 'grp')), may hold values from 0.25 to 1
Outputs:
- correction: float32 [3072, 128], P(('lead', 'grp'))
The draws below stay inside these ranges and needn't reach their ends.
Inputs may be any that keep to these rules, and one draw needn't show every extreme that they name: `tile_cols`: entry 0 of every row is that row's own block row within its leader, r for row l + r; indices below 1 are the leader's own block rows, the next 1 are the rows received from leader l - 1, the last 1 those received from leader l + 1 (cyclic). `send_rows`: the 1 entries of each list are distinct block rows of the sending leader.
All inputs are finite; a program needn't handle non-finite values.
Results may differ from the reference program's by a relative error of at most 0.0013.
Values may be sent and summed in bfloat16 or wider, within the bound.
A program may use at most 64 MiB of HBM per device.

```python
import math
import jax
import jax.numpy as jnp
from jax import lax

TILE = 384
TILES_ROW = 8
DEGREE = 2
NRHS = 128
GROUP_TILES = 8
BR_LEAD = 1
HALO = 1
EXT = 3
NDOF = 3072
NTILES = 64
N_LEAD = 8


def draw_tile_cols(key, part):
    row_total = N_LEAD * BR_LEAD
    picked = jax.random.randint(key, (row_total, TILES_ROW), 0, EXT, dtype=jnp.int32)
    local_row = jnp.arange(row_total, dtype=jnp.int32) % BR_LEAD
    slot_index = jnp.arange(TILES_ROW, dtype=jnp.int32)[None, :]
    picked = jnp.where(slot_index == 0, local_row[:, None], picked)
    corner_slot = (local_row[:, None] == 0) & (slot_index == TILES_ROW - 1)
    return jnp.where(corner_slot, EXT - 1, picked).astype(jnp.int32)


def draw_send_rows(key, part):
    key_list = jax.random.split(key, N_LEAD * 2)

    def one_order(one_key):
        return jax.random.permutation(one_key, BR_LEAD)
    orders = jax.vmap(one_order)(key_list)
    chosen = orders[:, :HALO].reshape(N_LEAD, 2, HALO).astype(jnp.int32)
    falling = (BR_LEAD - 1 - jnp.arange(HALO, dtype=jnp.int32)).astype(jnp.int32)
    rising = jnp.arange(HALO, dtype=jnp.int32)
    chosen = chosen.at[0, 0].set(falling).at[0, 1].set(rising)
    return chosen.astype(jnp.int32)


def shard_levels(rng, extent, shards, low, high):
    def one(position, blocks):
        heights = jax.random.uniform(jax.random.fold_in(jax.random.fold_in(rng, 6), position), (blocks,), jnp.float32, low / len(shards), high / len(shards))
        return jnp.repeat(jnp.exp(heights), extent[position] // blocks).reshape((-1,) + (1,) * (len(extent) - position - 1))

    loudness = one(*shards[0])
    for cut in shards[1:]:
        loudness = loudness * one(*cut)
    return loudness


def bell_draw(key, dims, spread, most, cuts=(), kind=jnp.bfloat16):
    result = jax.random.normal(key, dims, jnp.float32) * spread
    if len(cuts) > 0:
        result = shard_levels(key, dims, cuts, -0.22, 0.18) * result
    return jnp.clip(result, min=-most, max=most).astype(kind)


def setup_inputs(seed: int = 0) -> dict:
    arg_keys = jax.random.split(jax.random.key(seed), 7)
    matrix_tiles = bell_draw(arg_keys[0], (NTILES, TILE, TILE), (4 * TILE * TILES_ROW) ** -0.5, 0.0546875, ((0, 32),))
    tile_slot = jax.vmap(lambda own: jax.random.permutation(own, GROUP_TILES))(jax.random.split(arg_keys[1], N_LEAD)).reshape((N_LEAD, GROUP_TILES)).astype(jnp.int32)
    tile_cols = draw_tile_cols(jax.random.fold_in(arg_keys[6], 71), 0)
    send_rows = draw_send_rows(jax.random.fold_in(arg_keys[6], 71), 0)
    residual = bell_draw(arg_keys[4], (NDOF, NRHS), 1.0, 6.0, ((0, 32),), jnp.float32)
    diag_inv = jnp.clip(jnp.exp(math.log(1.0) - 1.3862944 * jax.random.uniform(arg_keys[5], (NDOF,), jnp.float32) ** shard_levels(arg_keys[5], (NDOF,), ((0, 32),), -0.2, 0.2)), 0.25, 1.0)
    return dict(matrix_tiles=matrix_tiles, tile_slot=tile_slot, tile_cols=tile_cols, send_rows=send_rows, residual=residual, diag_inv=diag_inv)


lower_bound = 0.5
upper_bound = 1.5


def coupling(vector, slot_tiles, tile_cols, send_rows):
    blocks = vector.astype(jnp.bfloat16).reshape(N_LEAD, BR_LEAD, TILE, NRHS)
    leaders = jnp.arange(N_LEAD, dtype=jnp.int32)
    lower_peer = (leaders - 1) % N_LEAD
    upper_peer = (leaders + 1) % N_LEAD
    from_lower = blocks[lower_peer[:, None], send_rows[lower_peer, 0]]
    from_upper = blocks[upper_peer[:, None], send_rows[upper_peer, 1]]
    extended = jnp.concatenate([blocks, from_lower, from_upper], axis=1)
    columns = tile_cols.reshape(N_LEAD, BR_LEAD, TILES_ROW)

    def one_leader(items):
        ext_rows, leader_tiles, leader_cols = items
        operand = ext_rows[leader_cols].astype(jnp.float32)
        return jnp.einsum("rkij,rkjn->rin", leader_tiles.astype(jnp.float32), operand,
                          precision=lax.Precision.HIGHEST)

    product = lax.map(one_leader, (extended, slot_tiles, columns))
    return product.reshape(NDOF, NRHS)


def one_sweep(start_residual, inverse, apply_operator):
    center_value = (upper_bound + lower_bound) / 2.0
    half_width = (upper_bound - lower_bound) / 2.0
    ratio_value = center_value / half_width
    update = inverse[:, None] * start_residual / center_value
    approx = update
    rho_now = 1.0 / ratio_value
    for repeat in range(DEGREE - 1):
        rho_next = 1.0 / (2.0 * ratio_value - rho_now)
        remaining = start_residual - apply_operator(approx)
        update = rho_next * rho_now * update + (2.0 * rho_next / half_width) * inverse[:, None] * remaining
        approx = approx + update
        rho_now = rho_next
    return approx


def reference(matrix_tiles, tile_slot, tile_cols, send_rows, residual, diag_inv):
    grouped = matrix_tiles.reshape(N_LEAD, GROUP_TILES, TILE, TILE)

    def place(items):
        leader_tiles, slots = items
        return jnp.zeros_like(leader_tiles).at[slots.astype(jnp.int32)].set(leader_tiles)

    slot_tiles = lax.map(place, (grouped, tile_slot)).reshape(N_LEAD, BR_LEAD, TILES_ROW, TILE, TILE)

    def apply_operator(approx):
        return approx / diag_inv[:, None] + coupling(approx, slot_tiles, tile_cols, send_rows)

    first_pass = one_sweep(residual, diag_inv, apply_operator)
    remaining = residual - apply_operator(first_pass)
    second_pass = one_sweep(remaining, diag_inv, apply_operator)
    return first_pass + second_pass
```

```python
import functools

import jax
import jax.numpy as jnp
from jax import lax
from jax.experimental import pallas as pl
from jax.experimental.pallas import tpu as pltpu
from jax.sharding import PartitionSpec as P

TILES_ROW = 8


lower_bound = 0.5
upper_bound = 1.5


def from_behind(shard, axis, by):
    devices = lax.axis_size(axis)
    return lax.ppermute(shard, axis, [(i, (i + by) % devices) for i in range(devices)])


def one_sweep(start_residual, inverse, apply_operator):
    center_value = (upper_bound + lower_bound) / 2.0
    half_width = (upper_bound - lower_bound) / 2.0
    ratio_value = center_value / half_width
    update = inverse[:, None] * start_residual / center_value
    approx = update
    rho_now = 1.0 / ratio_value
    rho_next = 1.0 / (2.0 * ratio_value - rho_now)
    remaining = start_residual - apply_operator(approx)
    update = (
        rho_next * rho_now * update + 2.0 * rho_next / half_width * inverse[:, None] * remaining
    )
    approx = approx + update
    return approx


def smooth_twice(rhs_field, inverse, apply_operator):
    first_pass = one_sweep(rhs_field, inverse, apply_operator)
    remaining = rhs_field - apply_operator(first_pass)
    second_pass = one_sweep(remaining, inverse, apply_operator)
    return first_pass + second_pass


def pick_blocks(blocks, rows):
    return jnp.concatenate(
        [lax.dynamic_slice_in_dim(blocks, rows[i], 1, 0) for i in range(rows.shape[0])], axis=0
    )


def extend(blocks, send_rows):
    position = lax.axis_index("lead")
    mine_up = pick_blocks(blocks, send_rows[position, 0])
    mine_down = pick_blocks(blocks, send_rows[position, 1])
    from_lower = from_behind(mine_up, "lead", 1)
    from_upper = from_behind(mine_down, "lead", -1)
    return jnp.concatenate([blocks, from_lower, from_upper], axis=0)


def local_general(matrix_tiles, tile_slot, tile_cols, send_rows, residual, diag_inv):
    block_rows = tile_cols.shape[0]
    tile_size = matrix_tiles.shape[1]
    member = lax.axis_index("grp")
    share_rows = residual.shape[0]
    group_slots = tile_slot[0]
    share_tiles = matrix_tiles.shape[0]
    members = lax.axis_size("grp")
    own_slots = lax.dynamic_slice_in_dim(group_slots, member * share_tiles, share_tiles, 0)
    own_block = own_slots // TILES_ROW
    target = jnp.arange(members, dtype=jnp.int32)[:, None, None]
    offsets = jnp.arange(share_rows, dtype=jnp.int32)[None, None, :]
    source_row = target * share_rows + offsets - own_block[None, :, None] * tile_size
    valid = (source_row >= 0) & (source_row < tile_size)
    clipped = jnp.clip(source_row, 0, tile_size - 1)
    tile_pick = jnp.arange(share_tiles, dtype=jnp.int32)[None, :, None]
    picked = matrix_tiles[tile_pick, clipped]
    outgoing = jnp.where(valid[..., None], picked, jnp.zeros_like(picked))
    received = lax.all_to_all(outgoing, "grp", split_axis=0, concat_axis=0, tiled=True)
    flat_rows = received.reshape(members * share_tiles, share_rows * tile_size)
    position_of = group_slots % TILES_ROW
    selector = (jnp.arange(TILES_ROW, dtype=jnp.int32)[:, None] == position_of[None, :]).astype(
        jnp.bfloat16
    )
    mine = jnp.dot(selector, flat_rows, preferred_element_type=jnp.float32).astype(jnp.bfloat16)
    mine = mine.reshape(TILES_ROW, share_rows, tile_size).transpose(1, 0, 2)
    mine = mine.reshape(share_rows, TILES_ROW * tile_size)
    first_block = member * share_rows // tile_size
    row_block = (member * share_rows + jnp.arange(share_rows, dtype=jnp.int32)) // tile_size

    def apply_operator(approx):
        rounded = approx.astype(jnp.bfloat16)
        gathered = lax.all_gather(rounded, "grp", axis=0, tiled=True)
        extended = extend(gathered.reshape(block_rows, tile_size, -1), send_rows)
        target_block = jnp.minimum(first_block + 0, block_rows - 1)
        operand = pick_blocks(extended, tile_cols[target_block])
        operand = operand.reshape(TILES_ROW * tile_size, -1)
        product = jnp.dot(mine, operand, preferred_element_type=jnp.float32)
        coupled = jnp.where((row_block == first_block + 0)[:, None], product, 0.0)
        return approx / diag_inv[:, None] + coupled

    correction = smooth_twice(residual, diag_inv, apply_operator)
    return correction


MESH = pl.DeviceIdType.MESH


def smoother_kernel(
    leads, members, slot_ref, cols_ref, tiles_ref, rhs_ref, inv_ref, out_ref,
    mine, ext0, ext1, ext2, local_sem, tile_send, tile_recv, send_sem, recv_sem,
):
    lead, me = lax.axis_index("lead"), lax.axis_index("grp")
    exts = (ext0, ext1, ext2)
    share_tiles, tile_size, _ = tiles_ref.shape
    rows, width = rhs_ref.shape
    total_tiles = share_tiles * members
    lower, upper = lax.rem(lead + leads - 1, leads), lax.rem(lead + 1, leads)
    others = [lax.rem(me + i, members) for i in range(1, members)]
    everyone = [me] + others

    partners = [(lead, p) for p in others]
    partners += [(lower, p) for p in everyone] + [(upper, p) for p in everyone]
    barrier = pltpu.get_barrier_semaphore()
    for partner in partners:
        pl.semaphore_signal(barrier, inc=1, device_id=partner, device_id_type=MESH)

    def rows_of(member):
        return pl.ds(pl.multiple_of(member * rows, rows), rows)

    def pieces(ext, block):
        return ext.at[block] if block else ext.at[0, pl.ds(0, (members - 1) * rows)]

    landing = mine.at[pl.ds(me * share_tiles, share_tiles)]
    own_copy = pltpu.make_async_copy(tiles_ref.at[:, rows_of(me), :], landing, local_sem)
    own_copy.start()

    row_id = lax.broadcasted_iota(jnp.int32, (rows, rows), 0)
    col_id = lax.broadcasted_iota(jnp.int32, (rows, rows), 1)
    inverse = jnp.broadcast_to(inv_ref[...], (rows, rows))
    inverse = jnp.sum(jnp.where(row_id == col_id, inverse, 0.0), axis=1, keepdims=True)
    rhs = rhs_ref[...]
    columns = [cols_ref[0, lax.rem(slot_ref[0, t], TILES_ROW)] for t in range(total_tiles)]

    def push(step, field):
        ext = exts[step]
        here = ext.at[0, rows_of(me), :]
        here[...] = field.astype(jnp.bfloat16)
        if step == 0:
            pl.semaphore_wait(barrier, len(partners))
            for p in others:
                pltpu.make_async_remote_copy(
                    src_ref=tiles_ref.at[:, rows_of(p), :], dst_ref=landing,
                    send_sem=tile_send, recv_sem=tile_recv,
                    device_id=(lead, p), device_id_type=MESH,
                ).start()
        for block, to_lead, targets in ((1, upper, everyone), (2, lower, everyone), (0, lead, others)):
            for p in targets:
                pltpu.make_async_remote_copy(
                    src_ref=here, dst_ref=ext.at[block, rows_of(me), :],
                    send_sem=send_sem.at[step, block], recv_sem=recv_sem.at[step, block],
                    device_id=(to_lead, p), device_id_type=MESH,
                ).start()

    def wait_for(ref, sem):
        pltpu.make_async_copy(ref, ref, sem).wait()

    def coupled(step):
        ext = exts[step]
        for block in range(3):
            wait_for(pieces(ext, block), recv_sem.at[step, block])
        if step == 0:
            own_copy.wait()
            wait_for(mine.at[pl.ds(0, (members - 1) * share_tiles)], tile_recv)
        left = jnp.concatenate([mine[t] for t in range(total_tiles)], axis=1)
        right = jnp.concatenate([ext[columns[t]] for t in range(total_tiles)], axis=0)
        return jnp.dot(left, right, preferred_element_type=jnp.float32)

    center = (upper_bound + lower_bound) / 2.0
    half = (upper_bound - lower_bound) / 2.0
    sigma = center / half
    rho = 1.0 / sigma
    rho_next = 1.0 / (2.0 * sigma - rho)
    keep, gain = 1.0 + rho_next * rho, 2.0 * rho_next / half
    rest = 1.0 - 1.0 / center

    def sweep(step, start):
        push(step, inverse * (start * (1.0 / center)))
        product = coupled(step)
        scaled = keep / center * start + gain * (rest * start - product)
        return inverse * scaled, scaled

    first, first_scaled = sweep(0, rhs)
    push(1, first)
    remaining = rhs - (first_scaled + coupled(1))
    second, _ = sweep(2, remaining)
    out_ref[...] = first + second

    wait_for(tiles_ref.at[:, pl.ds(0, (members - 1) * rows), :], tile_send)
    for step in range(3):
        for block in range(3):
            wait_for(pieces(exts[step], block), send_sem.at[step, block])


def local_kernel(leads, members, matrix_tiles, tile_slot, tile_cols, send_rows, residual, diag_inv):
    share_tiles, tile_size, _ = matrix_tiles.shape
    rows, width = residual.shape
    smem = pl.BlockSpec(memory_space=pltpu.SMEM)
    vmem = pl.BlockSpec(memory_space=pltpu.VMEM)
    work = 3 * 2 * rows * share_tiles * members * tile_size * width
    return pl.pallas_call(
        functools.partial(smoother_kernel, leads, members),
        out_shape=jax.ShapeDtypeStruct(residual.shape, residual.dtype),
        in_specs=[smem, smem, pl.BlockSpec(memory_space=pl.ANY), vmem, vmem],
        out_specs=vmem,
        scratch_shapes=[
            pltpu.VMEM((members * share_tiles, rows, tile_size), jnp.bfloat16),
            *[pltpu.VMEM((3, tile_size, width), jnp.bfloat16)] * 3,
            pltpu.SemaphoreType.DMA,
            pltpu.SemaphoreType.DMA,
            pltpu.SemaphoreType.DMA,
            pltpu.SemaphoreType.DMA((3, 3)),
            pltpu.SemaphoreType.DMA((3, 3)),
        ],
        cost_estimate=pl.CostEstimate(
            flops=work, bytes_accessed=matrix_tiles.size * 2 + residual.size * 8, transcendentals=0
        ),
        compiler_params=pltpu.CompilerParams(
            collective_id=0, has_side_effects=True, vmem_limit_bytes=24 * 1024 * 1024
        ),
    )(tile_slot, tile_cols, matrix_tiles, residual, diag_inv.reshape(1, rows))


def local(*args):
    leads, members = lax.axis_size("lead"), lax.axis_size("grp")
    if args[2].shape[0] == 1 and leads > 2 and members > 1:
        return local_kernel(leads, members, *args)
    return local_general(*args)


def solution(mesh):
    in_specs = (
        P(("lead", "grp"), None, None),
        P("lead", None),
        P("lead", None),
        P(),
        P(("lead", "grp"), None),
        P(("lead", "grp")),
    )
    out_specs = P(("lead", "grp"), None)
    return jax.shard_map(local, mesh=mesh, in_specs=in_specs, out_specs=out_specs, check_vma=False)
```

```python
import functools

import jax
import jax.numpy as jnp
from jax import lax
from jax.experimental import pallas as pl
from jax.experimental.pallas import tpu as pltpu
from jax.sharding import PartitionSpec as P

TILES_ROW = 8


lower_bound = 0.5
upper_bound = 1.5


def from_behind(shard, axis, by):
    devices = lax.axis_size(axis)
    return lax.ppermute(shard, axis, [(i, (i + by) % devices) for i in range(devices)])


def one_sweep(start_residual, inverse, apply_operator):
    center_value = (upper_bound + lower_bound) / 2.0
    half_width = (upper_bound - lower_bound) / 2.0
    ratio_value = center_value / half_width
    update = inverse[:, None] * start_residual / center_value
    approx = update
    rho_now = 1.0 / ratio_value
    rho_next = 1.0 / (2.0 * ratio_value - rho_now)
    remaining = start_residual - apply_operator(approx)
    update = (
        rho_next * rho_now * update + 2.0 * rho_next / half_width * inverse[:, None] * remaining
    )
    approx = approx + update
    return approx


def smooth_twice(rhs_field, inverse, apply_operator):
    first_pass = one_sweep(rhs_field, inverse, apply_operator)
    remaining = rhs_field - apply_operator(first_pass)
    second_pass = one_sweep(remaining, inverse, apply_operator)
    return first_pass + second_pass


def pick_blocks(blocks, rows):
    return jnp.concatenate(
        [lax.dynamic_slice_in_dim(blocks, rows[i], 1, 0) for i in range(rows.shape[0])], axis=0
    )


def extend(blocks, send_rows):
    position = lax.axis_index("lead")
    mine_up = pick_blocks(blocks, send_rows[position, 0])
    mine_down = pick_blocks(blocks, send_rows[position, 1])
    from_lower = from_behind(mine_up, "lead", 1)
    from_upper = from_behind(mine_down, "lead", -1)
    return jnp.concatenate([blocks, from_lower, from_upper], axis=0)


def local_general(matrix_tiles, tile_slot, tile_cols, send_rows, residual, diag_inv):
    block_rows = tile_cols.shape[0]
    tile_size = matrix_tiles.shape[1]
    member = lax.axis_index("grp")
    share_rows = residual.shape[0]
    group_slots = tile_slot[0]
    share_tiles = matrix_tiles.shape[0]
    members = lax.axis_size("grp")
    own_slots = lax.dynamic_slice_in_dim(group_slots, member * share_tiles, share_tiles, 0)
    own_block = own_slots // TILES_ROW
    target = jnp.arange(members, dtype=jnp.int32)[:, None, None]
    offsets = jnp.arange(share_rows, dtype=jnp.int32)[None, None, :]
    source_row = target * share_rows + offsets - own_block[None, :, None] * tile_size
    valid = (source_row >= 0) & (source_row < tile_size)
    clipped = jnp.clip(source_row, 0, tile_size - 1)
    tile_pick = jnp.arange(share_tiles, dtype=jnp.int32)[None, :, None]
    picked = matrix_tiles[tile_pick, clipped]
    outgoing = jnp.where(valid[..., None], picked, jnp.zeros_like(picked))
    received = lax.all_to_all(outgoing, "grp", split_axis=0, concat_axis=0, tiled=True)
    flat_rows = received.reshape(members * share_tiles, share_rows * tile_size)
    position_of = group_slots % TILES_ROW
    selector = (jnp.arange(TILES_ROW, dtype=jnp.int32)[:, None] == position_of[None, :]).astype(
        jnp.bfloat16
    )
    mine = jnp.dot(selector, flat_rows, preferred_element_type=jnp.float32).astype(jnp.bfloat16)
    mine = mine.reshape(TILES_ROW, share_rows, tile_size).transpose(1, 0, 2)
    mine = mine.reshape(share_rows, TILES_ROW * tile_size)
    first_block = member * share_rows // tile_size
    row_block = (member * share_rows + jnp.arange(share_rows, dtype=jnp.int32)) // tile_size

    def apply_operator(approx):
        rounded = approx.astype(jnp.bfloat16)
        gathered = lax.all_gather(rounded, "grp", axis=0, tiled=True)
        extended = extend(gathered.reshape(block_rows, tile_size, -1), send_rows)
        target_block = jnp.minimum(first_block + 0, block_rows - 1)
        operand = pick_blocks(extended, tile_cols[target_block])
        operand = operand.reshape(TILES_ROW * tile_size, -1)
        product = jnp.dot(mine, operand, preferred_element_type=jnp.float32)
        coupled = jnp.where((row_block == first_block + 0)[:, None], product, 0.0)
        return approx / diag_inv[:, None] + coupled

    correction = smooth_twice(residual, diag_inv, apply_operator)
    return correction


MESH = pl.DeviceIdType.MESH


def smoother_kernel(
    leads, members, slot_ref, cols_ref, tiles_ref, rhs_in, inv_in, out_ref,
    rhs_ref, inv_ref, mine, ext0, ext1, ext2, local_sem, tile_send, tile_recv, send_sem, recv_sem,
):
    lead, me = lax.axis_index("lead"), lax.axis_index("grp")
    exts = (ext0, ext1, ext2)
    share_tiles, tile_size, _ = tiles_ref.shape
    rows, width = rhs_in.shape
    total_tiles = share_tiles * members
    lower, upper = lax.rem(lead + leads - 1, leads), lax.rem(lead + 1, leads)
    others = [lax.rem(me + i, members) for i in range(1, members)]
    everyone = [me] + others

    partners = [(lead, p) for p in others]
    partners += [(lower, p) for p in everyone] + [(upper, p) for p in everyone]
    barrier = pltpu.get_barrier_semaphore()
    for partner in partners:
        pl.semaphore_signal(barrier, inc=1, device_id=partner, device_id_type=MESH)

    def rows_of(member):
        return pl.ds(pl.multiple_of(member * rows, rows), rows)

    def pieces(ext, block):
        return ext.at[block] if block else ext.at[0, pl.ds(0, (members - 1) * rows)]

    landing = mine.at[pl.ds(me * share_tiles, share_tiles)]
    load_rhs = pltpu.make_async_copy(rhs_in, rhs_ref, local_sem.at[0])
    load_rhs.start()
    load_inv = pltpu.make_async_copy(inv_in, inv_ref, local_sem.at[1])
    load_inv.start()
    own_copy = pltpu.make_async_copy(tiles_ref.at[:, rows_of(me), :], landing, local_sem.at[2])
    own_copy.start()
    columns = [cols_ref[0, lax.rem(slot_ref[0, t], TILES_ROW)] for t in range(total_tiles)]

    pl.semaphore_wait(barrier, len(partners))
    for p in others:
        pltpu.make_async_remote_copy(
            src_ref=tiles_ref.at[:, rows_of(p), :], dst_ref=landing,
            send_sem=tile_send, recv_sem=tile_recv,
            device_id=(lead, p), device_id_type=MESH,
        ).start()
    load_rhs.wait()
    load_inv.wait()

    row_id = lax.broadcasted_iota(jnp.int32, (rows, rows), 0)
    col_id = lax.broadcasted_iota(jnp.int32, (rows, rows), 1)
    inverse = jnp.broadcast_to(inv_ref[...], (rows, rows))
    inverse = jnp.sum(jnp.where(row_id == col_id, inverse, 0.0), axis=1, keepdims=True)
    rhs = rhs_ref[...]

    def push(step, field):
        ext = exts[step]
        here = ext.at[0, rows_of(me), :]
        here[...] = field.astype(jnp.bfloat16)
        for block, to_lead, targets in ((1, upper, everyone), (2, lower, everyone), (0, lead, others)):
            for p in targets:
                pltpu.make_async_remote_copy(
                    src_ref=here, dst_ref=ext.at[block, rows_of(me), :],
                    send_sem=send_sem.at[step, block], recv_sem=recv_sem.at[step, block],
                    device_id=(to_lead, p), device_id_type=MESH,
                ).start()

    def wait_for(ref, sem):
        pltpu.make_async_copy(ref, ref, sem).wait()

    def coupled(step):
        ext = exts[step]
        for block in range(3):
            wait_for(pieces(ext, block), recv_sem.at[step, block])
        if step == 0:
            own_copy.wait()
            wait_for(mine.at[pl.ds(0, (members - 1) * share_tiles)], tile_recv)
        left = jnp.concatenate([mine[t] for t in range(total_tiles)], axis=1)
        right = jnp.concatenate([ext[columns[t]] for t in range(total_tiles)], axis=0)
        return jnp.dot(left, right, preferred_element_type=jnp.float32)

    center = (upper_bound + lower_bound) / 2.0
    half = (upper_bound - lower_bound) / 2.0
    sigma = center / half
    rho = 1.0 / sigma
    rho_next = 1.0 / (2.0 * sigma - rho)
    keep, gain = 1.0 + rho_next * rho, 2.0 * rho_next / half
    rest = 1.0 - 1.0 / center

    def sweep(step, start):
        push(step, inverse * (start * (1.0 / center)))
        product = coupled(step)
        scaled = keep / center * start + gain * (rest * start - product)
        return inverse * scaled, scaled

    first, first_scaled = sweep(0, rhs)
    push(1, first)
    remaining = rhs - (first_scaled + coupled(1))
    second, _ = sweep(2, remaining)
    out_ref[...] = first + second

    wait_for(tiles_ref.at[:, pl.ds(0, (members - 1) * rows), :], tile_send)
    for step in range(3):
        for block in range(3):
            wait_for(pieces(exts[step], block), send_sem.at[step, block])


def local_kernel(leads, members, matrix_tiles, tile_slot, tile_cols, send_rows, residual, diag_inv):
    share_tiles, tile_size, _ = matrix_tiles.shape
    rows, width = residual.shape
    smem = pl.BlockSpec(memory_space=pltpu.SMEM)
    vmem = pl.BlockSpec(memory_space=pltpu.VMEM)
    anywhere = pl.BlockSpec(memory_space=pl.ANY)
    work = 3 * 2 * rows * share_tiles * members * tile_size * width
    return pl.pallas_call(
        functools.partial(smoother_kernel, leads, members),
        out_shape=jax.ShapeDtypeStruct(residual.shape, residual.dtype),
        in_specs=[smem, smem, anywhere, anywhere, anywhere],
        out_specs=vmem,
        scratch_shapes=[
            pltpu.VMEM((rows, width), residual.dtype),
            pltpu.VMEM((1, rows), diag_inv.dtype),
            pltpu.VMEM((members * share_tiles, rows, tile_size), jnp.bfloat16),
            *[pltpu.VMEM((3, tile_size, width), jnp.bfloat16)] * 3,
            pltpu.SemaphoreType.DMA((3,)),
            pltpu.SemaphoreType.DMA,
            pltpu.SemaphoreType.DMA,
            pltpu.SemaphoreType.DMA((3, 3)),
            pltpu.SemaphoreType.DMA((3, 3)),
        ],
        cost_estimate=pl.CostEstimate(
            flops=work, bytes_accessed=matrix_tiles.size * 2 + residual.size * 8, transcendentals=0
        ),
        compiler_params=pltpu.CompilerParams(
            collective_id=0, has_side_effects=True, vmem_limit_bytes=60 * 1024 * 1024
        ),
    )(tile_slot, tile_cols, matrix_tiles, residual, diag_inv.reshape(1, rows))


def local(*args):
    leads, members = lax.axis_size("lead"), lax.axis_size("grp")
    if args[2].shape[0] == 1 and leads > 2 and members > 1:
        return local_kernel(leads, members, *args)
    return local_general(*args)


def solution(mesh):
    in_specs = (
        P(("lead", "grp"), None, None),
        P("lead", None),
        P("lead", None),
        P(),
        P(("lead", "grp"), None),
        P(("lead", "grp")),
    )
    out_specs = P(("lead", "grp"), None)
    return jax.shard_map(local, mesh=mesh, in_specs=in_specs, out_specs=out_specs, check_vma=False)
```

```python
import functools

import jax
import jax.numpy as jnp
from jax import lax
from jax.experimental import pallas as pl
from jax.experimental.pallas import tpu as pltpu
from jax.sharding import PartitionSpec as P

TILES_ROW = 8


lower_bound = 0.5
upper_bound = 1.5


def from_behind(shard, axis, by):
    devices = lax.axis_size(axis)
    return lax.ppermute(shard, axis, [(i, (i + by) % devices) for i in range(devices)])


def one_sweep(start_residual, inverse, apply_operator):
    center_value = (upper_bound + lower_bound) / 2.0
    half_width = (upper_bound - lower_bound) / 2.0
    ratio_value = center_value / half_width
    update = inverse[:, None] * start_residual / center_value
    approx = update
    rho_now = 1.0 / ratio_value
    rho_next = 1.0 / (2.0 * ratio_value - rho_now)
    remaining = start_residual - apply_operator(approx)
    update = (
        rho_next * rho_now * update + 2.0 * rho_next / half_width * inverse[:, None] * remaining
    )
    approx = approx + update
    return approx


def smooth_twice(rhs_field, inverse, apply_operator):
    first_pass = one_sweep(rhs_field, inverse, apply_operator)
    remaining = rhs_field - apply_operator(first_pass)
    second_pass = one_sweep(remaining, inverse, apply_operator)
    return first_pass + second_pass


def pick_blocks(blocks, rows):
    return jnp.concatenate(
        [lax.dynamic_slice_in_dim(blocks, rows[i], 1, 0) for i in range(rows.shape[0])], axis=0
    )


def extend(blocks, send_rows):
    position = lax.axis_index("lead")
    mine_up = pick_blocks(blocks, send_rows[position, 0])
    mine_down = pick_blocks(blocks, send_rows[position, 1])
    from_lower = from_behind(mine_up, "lead", 1)
    from_upper = from_behind(mine_down, "lead", -1)
    return jnp.concatenate([blocks, from_lower, from_upper], axis=0)


def local_general(matrix_tiles, tile_slot, tile_cols, send_rows, residual, diag_inv):
    block_rows = tile_cols.shape[0]
    tile_size = matrix_tiles.shape[1]
    member = lax.axis_index("grp")
    share_rows = residual.shape[0]
    group_slots = tile_slot[0]
    share_tiles = matrix_tiles.shape[0]
    members = lax.axis_size("grp")
    own_slots = lax.dynamic_slice_in_dim(group_slots, member * share_tiles, share_tiles, 0)
    own_block = own_slots // TILES_ROW
    target = jnp.arange(members, dtype=jnp.int32)[:, None, None]
    offsets = jnp.arange(share_rows, dtype=jnp.int32)[None, None, :]
    source_row = target * share_rows + offsets - own_block[None, :, None] * tile_size
    valid = (source_row >= 0) & (source_row < tile_size)
    clipped = jnp.clip(source_row, 0, tile_size - 1)
    tile_pick = jnp.arange(share_tiles, dtype=jnp.int32)[None, :, None]
    picked = matrix_tiles[tile_pick, clipped]
    outgoing = jnp.where(valid[..., None], picked, jnp.zeros_like(picked))
    received = lax.all_to_all(outgoing, "grp", split_axis=0, concat_axis=0, tiled=True)
    flat_rows = received.reshape(members * share_tiles, share_rows * tile_size)
    position_of = group_slots % TILES_ROW
    selector = (jnp.arange(TILES_ROW, dtype=jnp.int32)[:, None] == position_of[None, :]).astype(
        jnp.bfloat16
    )
    mine = jnp.dot(selector, flat_rows, preferred_element_type=jnp.float32).astype(jnp.bfloat16)
    mine = mine.reshape(TILES_ROW, share_rows, tile_size).transpose(1, 0, 2)
    mine = mine.reshape(share_rows, TILES_ROW * tile_size)
    first_block = member * share_rows // tile_size
    row_block = (member * share_rows + jnp.arange(share_rows, dtype=jnp.int32)) // tile_size

    def apply_operator(approx):
        rounded = approx.astype(jnp.bfloat16)
        gathered = lax.all_gather(rounded, "grp", axis=0, tiled=True)
        extended = extend(gathered.reshape(block_rows, tile_size, -1), send_rows)
        target_block = jnp.minimum(first_block + 0, block_rows - 1)
        operand = pick_blocks(extended, tile_cols[target_block])
        operand = operand.reshape(TILES_ROW * tile_size, -1)
        product = jnp.dot(mine, operand, preferred_element_type=jnp.float32)
        coupled = jnp.where((row_block == first_block + 0)[:, None], product, 0.0)
        return approx / diag_inv[:, None] + coupled

    correction = smooth_twice(residual, diag_inv, apply_operator)
    return correction


MESH = pl.DeviceIdType.MESH


def smoother_kernel(
    leads, members, slot_ref, cols_ref, tiles_ref, rhs_in, inv_in, out_ref,
    rhs_ref, inv_ref, mine, ext0, ext1, ext2, local_sem, tile_send, tile_recv, send_sem, recv_sem,
):
    lead, me = lax.axis_index("lead"), lax.axis_index("grp")
    exts = (ext0, ext1, ext2)
    share_tiles, tile_size, _ = tiles_ref.shape
    rows, width = rhs_in.shape
    total_tiles = share_tiles * members
    lower, upper = lax.rem(lead + leads - 1, leads), lax.rem(lead + 1, leads)
    others = [lax.rem(me + i, members) for i in range(1, members)]
    everyone = [me] + others

    partners = [(lead, p) for p in others]
    partners += [(lower, p) for p in everyone] + [(upper, p) for p in everyone]
    barrier = pltpu.get_barrier_semaphore()
    for partner in partners:
        pl.semaphore_signal(barrier, inc=1, device_id=partner, device_id_type=MESH)

    def rows_of(member):
        return pl.ds(pl.multiple_of(member * rows, rows), rows)

    def pieces(ext, block):
        return ext.at[block] if block else ext.at[0, pl.ds(0, (members - 1) * rows)]

    landing = mine.at[pl.ds(me * share_tiles, share_tiles)]
    load_rhs = pltpu.make_async_copy(rhs_in, rhs_ref, local_sem.at[0])
    load_rhs.start()
    load_inv = pltpu.make_async_copy(inv_in, inv_ref, local_sem.at[1])
    load_inv.start()
    own_copy = pltpu.make_async_copy(tiles_ref.at[:, rows_of(me), :], landing, local_sem.at[2])
    own_copy.start()
    columns = [cols_ref[0, lax.rem(slot_ref[0, t], TILES_ROW)] for t in range(total_tiles)]

    pl.semaphore_wait(barrier, len(partners))
    for p in others:
        pltpu.make_async_remote_copy(
            src_ref=tiles_ref.at[:, rows_of(p), :], dst_ref=landing,
            send_sem=tile_send, recv_sem=tile_recv,
            device_id=(lead, p), device_id_type=MESH,
        ).start()
    load_rhs.wait()
    load_inv.wait()

    row_id = lax.broadcasted_iota(jnp.int32, (rows, rows), 0)
    col_id = lax.broadcasted_iota(jnp.int32, (rows, rows), 1)
    inverse = jnp.broadcast_to(inv_ref[...], (rows, rows))
    inverse = jnp.sum(jnp.where(row_id == col_id, inverse, 0.0), axis=1, keepdims=True)
    rhs = rhs_ref[...]

    def push(step, field):
        ext = exts[step]
        here = ext.at[0, rows_of(me), :]
        here[...] = field.astype(jnp.bfloat16)
        for block, to_lead, targets in ((1, upper, everyone), (2, lower, everyone), (0, lead, others)):
            for p in targets:
                pltpu.make_async_remote_copy(
                    src_ref=here, dst_ref=ext.at[block, rows_of(me), :],
                    send_sem=send_sem.at[step, block], recv_sem=recv_sem.at[step, block],
                    device_id=(to_lead, p), device_id_type=MESH,
                ).start()

    def wait_for(ref, sem):
        pltpu.make_async_copy(ref, ref, sem).wait()

    def coupled(step):
        ext = exts[step]
        for block in range(3):
            wait_for(pieces(ext, block), recv_sem.at[step, block])
        if step == 0:
            own_copy.wait()
            wait_for(mine.at[pl.ds(0, (members - 1) * share_tiles)], tile_recv)
        left = jnp.concatenate([mine[t] for t in range(total_tiles)], axis=1)
        right = jnp.concatenate([ext[columns[t]] for t in range(total_tiles)], axis=0)
        return jnp.dot(left, right, preferred_element_type=jnp.float32)

    center = (upper_bound + lower_bound) / 2.0
    half = (upper_bound - lower_bound) / 2.0
    sigma = center / half
    rho = 1.0 / sigma
    rho_next = 1.0 / (2.0 * sigma - rho)
    keep, gain = 1.0 + rho_next * rho, 2.0 * rho_next / half
    rest = 1.0 - 1.0 / center

    def sweep(step, start):
        push(step, inverse * (start * (1.0 / center)))
        product = coupled(step)
        scaled = keep / center * start + gain * (rest * start - product)
        return inverse * scaled, scaled

    first, first_scaled = sweep(0, rhs)
    push(1, first)
    remaining = rhs - (first_scaled + coupled(1))
    second, _ = sweep(2, remaining)
    out_ref[...] = first + second

    wait_for(tiles_ref.at[:, pl.ds(0, (members - 1) * rows), :], tile_send)
    for step in range(3):
        for block in range(3):
            wait_for(pieces(exts[step], block), send_sem.at[step, block])


def local_kernel(leads, members, matrix_tiles, tile_slot, tile_cols, send_rows, residual, diag_inv):
    share_tiles, tile_size, _ = matrix_tiles.shape
    rows, width = residual.shape
    smem = pl.BlockSpec(memory_space=pltpu.SMEM)
    vmem = pl.BlockSpec(memory_space=pltpu.VMEM)
    anywhere = pl.BlockSpec(memory_space=pltpu.HBM)
    work = 3 * 2 * rows * share_tiles * members * tile_size * width
    return pl.pallas_call(
        functools.partial(smoother_kernel, leads, members),
        out_shape=jax.ShapeDtypeStruct(residual.shape, residual.dtype),
        in_specs=[smem, smem, anywhere, anywhere, anywhere],
        out_specs=vmem,
        scratch_shapes=[
            pltpu.VMEM((rows, width), residual.dtype),
            pltpu.VMEM((1, rows), diag_inv.dtype),
            pltpu.VMEM((members * share_tiles, rows, tile_size), jnp.bfloat16),
            *[pltpu.VMEM((3, tile_size, width), jnp.bfloat16)] * 3,
            pltpu.SemaphoreType.DMA((3,)),
            pltpu.SemaphoreType.DMA,
            pltpu.SemaphoreType.DMA,
            pltpu.SemaphoreType.DMA((3, 3)),
            pltpu.SemaphoreType.DMA((3, 3)),
        ],
        cost_estimate=pl.CostEstimate(
            flops=work, bytes_accessed=matrix_tiles.size * 2 + residual.size * 8, transcendentals=0
        ),
        compiler_params=pltpu.CompilerParams(
            collective_id=0, has_side_effects=True, vmem_limit_bytes=24 * 1024 * 1024
        ),
    )(tile_slot, tile_cols, matrix_tiles, residual, diag_inv.reshape(1, rows))


def local(*args):
    leads, members = lax.axis_size("lead"), lax.axis_size("grp")
    if args[2].shape[0] == 1 and leads > 2 and members > 1:
        return local_kernel(leads, members, *args)
    return local_general(*args)


def solution(mesh):
    in_specs = (
        P(("lead", "grp"), None, None),
        P("lead", None),
        P("lead", None),
        P(),
        P(("lead", "grp"), None),
        P(("lead", "grp")),
    )
    out_specs = P(("lead", "grp"), None)
    return jax.shard_map(local, mesh=mesh, in_specs=in_specs, out_specs=out_specs, check_vma=False)
```

```python
import functools

import jax
import jax.numpy as jnp
from jax import lax
from jax.experimental import pallas as pl
from jax.experimental.pallas import tpu as pltpu
from jax.sharding import PartitionSpec as P

TILES_ROW = 8


lower_bound = 0.5
upper_bound = 1.5


def from_behind(shard, axis, by):
    devices = lax.axis_size(axis)
    return lax.ppermute(shard, axis, [(i, (i + by) % devices) for i in range(devices)])


def one_sweep(start_residual, inverse, apply_operator):
    center_value = (upper_bound + lower_bound) / 2.0
    half_width = (upper_bound - lower_bound) / 2.0
    ratio_value = center_value / half_width
    update = inverse[:, None] * start_residual / center_value
    approx = update
    rho_now = 1.0 / ratio_value
    rho_next = 1.0 / (2.0 * ratio_value - rho_now)
    remaining = start_residual - apply_operator(approx)
    update = (
        rho_next * rho_now * update + 2.0 * rho_next / half_width * inverse[:, None] * remaining
    )
    approx = approx + update
    return approx


def smooth_twice(rhs_field, inverse, apply_operator):
    first_pass = one_sweep(rhs_field, inverse, apply_operator)
    remaining = rhs_field - apply_operator(first_pass)
    second_pass = one_sweep(remaining, inverse, apply_operator)
    return first_pass + second_pass


def pick_blocks(blocks, rows):
    return jnp.concatenate(
        [lax.dynamic_slice_in_dim(blocks, rows[i], 1, 0) for i in range(rows.shape[0])], axis=0
    )


def extend(blocks, send_rows):
    position = lax.axis_index("lead")
    mine_up = pick_blocks(blocks, send_rows[position, 0])
    mine_down = pick_blocks(blocks, send_rows[position, 1])
    from_lower = from_behind(mine_up, "lead", 1)
    from_upper = from_behind(mine_down, "lead", -1)
    return jnp.concatenate([blocks, from_lower, from_upper], axis=0)


def local_general(matrix_tiles, tile_slot, tile_cols, send_rows, residual, diag_inv):
    block_rows = tile_cols.shape[0]
    tile_size = matrix_tiles.shape[1]
    member = lax.axis_index("grp")
    share_rows = residual.shape[0]
    group_slots = tile_slot[0]
    share_tiles = matrix_tiles.shape[0]
    members = lax.axis_size("grp")
    own_slots = lax.dynamic_slice_in_dim(group_slots, member * share_tiles, share_tiles, 0)
    own_block = own_slots // TILES_ROW
    target = jnp.arange(members, dtype=jnp.int32)[:, None, None]
    offsets = jnp.arange(share_rows, dtype=jnp.int32)[None, None, :]
    source_row = target * share_rows + offsets - own_block[None, :, None] * tile_size
    valid = (source_row >= 0) & (source_row < tile_size)
    clipped = jnp.clip(source_row, 0, tile_size - 1)
    tile_pick = jnp.arange(share_tiles, dtype=jnp.int32)[None, :, None]
    picked = matrix_tiles[tile_pick, clipped]
    outgoing = jnp.where(valid[..., None], picked, jnp.zeros_like(picked))
    received = lax.all_to_all(outgoing, "grp", split_axis=0, concat_axis=0, tiled=True)
    flat_rows = received.reshape(members * share_tiles, share_rows * tile_size)
    position_of = group_slots % TILES_ROW
    selector = (jnp.arange(TILES_ROW, dtype=jnp.int32)[:, None] == position_of[None, :]).astype(
        jnp.bfloat16
    )
    mine = jnp.dot(selector, flat_rows, preferred_element_type=jnp.float32).astype(jnp.bfloat16)
    mine = mine.reshape(TILES_ROW, share_rows, tile_size).transpose(1, 0, 2)
    mine = mine.reshape(share_rows, TILES_ROW * tile_size)
    first_block = member * share_rows // tile_size
    row_block = (member * share_rows + jnp.arange(share_rows, dtype=jnp.int32)) // tile_size

    def apply_operator(approx):
        rounded = approx.astype(jnp.bfloat16)
        gathered = lax.all_gather(rounded, "grp", axis=0, tiled=True)
        extended = extend(gathered.reshape(block_rows, tile_size, -1), send_rows)
        target_block = jnp.minimum(first_block + 0, block_rows - 1)
        operand = pick_blocks(extended, tile_cols[target_block])
        operand = operand.reshape(TILES_ROW * tile_size, -1)
        product = jnp.dot(mine, operand, preferred_element_type=jnp.float32)
        coupled = jnp.where((row_block == first_block + 0)[:, None], product, 0.0)
        return approx / diag_inv[:, None] + coupled

    correction = smooth_twice(residual, diag_inv, apply_operator)
    return correction


MESH = pl.DeviceIdType.MESH


def smoother_kernel(
    leads, members, slot_ref, cols_ref, tiles_ref, rhs_in, inv_in, out_ref,
    rhs_ref, inv_ref, mine, ext0, ext1, ext2, local_sem, tile_send, tile_recv, send_sem, recv_sem, group_sem,
):
    lead, me = lax.axis_index("lead"), lax.axis_index("grp")
    exts = (ext0, ext1, ext2)
    share_tiles, tile_size, _ = tiles_ref.shape
    rows, width = rhs_in.shape
    total_tiles = share_tiles * members
    odd = lax.rem(lead, 2)
    mate = lead + 1 - 2 * odd
    far = lax.rem(lead + leads - 1 + 2 * odd, leads)
    at_mate, at_far = 1 + odd, 2 - odd
    others = [lax.rem(me + i, members) for i in range(1, members)]
    everyone = [me] + others

    partners = [(lead, p) for p in others]
    partners += [(far, p) for p in everyone] + [(mate, me)]
    barrier = pltpu.get_barrier_semaphore()
    for partner in partners:
        pl.semaphore_signal(barrier, inc=1, device_id=partner, device_id_type=MESH)

    def rows_of(member):
        return pl.ds(pl.multiple_of(member * rows, rows), rows)

    def pieces(ext, block):
        return ext.at[block] if block else ext.at[0, pl.ds(0, (members - 1) * rows)]

    landing = mine.at[pl.ds(me * share_tiles, share_tiles)]
    load_rhs = pltpu.make_async_copy(rhs_in, rhs_ref, local_sem.at[0])
    load_rhs.start()
    load_inv = pltpu.make_async_copy(inv_in, inv_ref, local_sem.at[1])
    load_inv.start()
    own_copy = pltpu.make_async_copy(tiles_ref.at[:, rows_of(me), :], landing, local_sem.at[2])
    own_copy.start()
    columns = [cols_ref[0, lax.rem(slot_ref[0, t], TILES_ROW)] for t in range(total_tiles)]

    load_rhs.wait()
    load_inv.wait()

    row_id = lax.broadcasted_iota(jnp.int32, (rows, rows), 0)
    col_id = lax.broadcasted_iota(jnp.int32, (rows, rows), 1)
    inverse = jnp.broadcast_to(inv_ref[...], (rows, rows))
    inverse = jnp.sum(jnp.where(row_id == col_id, inverse, 0.0), axis=1, keepdims=True)
    rhs = rhs_ref[...]

    def push(step, field):
        ext = exts[step]
        here = ext.at[0, rows_of(me), :]
        here[...] = field.astype(jnp.bfloat16)
        if step == 0:
            pl.semaphore_wait(barrier, len(partners))
        for i, p in enumerate(others):
            pltpu.make_async_remote_copy(
                src_ref=here, dst_ref=here,
                send_sem=send_sem.at[step, 0], recv_sem=group_sem.at[step, i],
                device_id=(lead, p), device_id_type=MESH,
            ).start()
        for p in everyone:
            pltpu.make_async_remote_copy(
                src_ref=here, dst_ref=ext.at[at_far, rows_of(me), :],
                send_sem=send_sem.at[step, 1], recv_sem=recv_sem.at[step, at_far],
                device_id=(far, p), device_id_type=MESH,
            ).start()
        pass_on(step, me)
        if step == 0:
            for p in others:
                pltpu.make_async_remote_copy(
                    src_ref=tiles_ref.at[:, rows_of(p), :], dst_ref=landing,
                    send_sem=tile_send, recv_sem=tile_recv,
                    device_id=(lead, p), device_id_type=MESH,
                ).start()

    def pass_on(step, owner):
        ext = exts[step]
        pltpu.make_async_remote_copy(
            src_ref=ext.at[0, rows_of(owner), :], dst_ref=ext.at[at_mate, rows_of(owner), :],
            send_sem=send_sem.at[step, 2], recv_sem=recv_sem.at[step, at_mate],
            device_id=(mate, me), device_id_type=MESH,
        ).start()

    def wait_for(ref, sem):
        pltpu.make_async_copy(ref, ref, sem).wait()

    def coupled(step):
        ext = exts[step]
        for i in range(1, members):
            owner = lax.rem(me + members - i, members)
            wait_for(ext.at[0, rows_of(owner), :], group_sem.at[step, i - 1])
            pass_on(step, owner)
        for block in (1, 2):
            wait_for(ext.at[block], recv_sem.at[step, block])
        if step == 0:
            own_copy.wait()
            wait_for(mine.at[pl.ds(0, (members - 1) * share_tiles)], tile_recv)
        left = jnp.concatenate([mine[t] for t in range(total_tiles)], axis=1)
        right = jnp.concatenate([ext[columns[t]] for t in range(total_tiles)], axis=0)
        return jnp.dot(left, right, preferred_element_type=jnp.float32)

    center = (upper_bound + lower_bound) / 2.0
    half = (upper_bound - lower_bound) / 2.0
    sigma = center / half
    rho = 1.0 / sigma
    rho_next = 1.0 / (2.0 * sigma - rho)
    keep, gain = 1.0 + rho_next * rho, 2.0 * rho_next / half
    rest = 1.0 - 1.0 / center

    def sweep(step, start):
        push(step, inverse * (start * (1.0 / center)))
        product = coupled(step)
        scaled = keep / center * start + gain * (rest * start - product)
        return inverse * scaled, scaled

    first, first_scaled = sweep(0, rhs)
    push(1, first)
    remaining = rhs - (first_scaled + coupled(1))
    second, _ = sweep(2, remaining)
    out_ref[...] = first + second

    wait_for(tiles_ref.at[:, pl.ds(0, (members - 1) * rows), :], tile_send)
    for step in range(3):
        for block in range(3):
            wait_for(pieces(exts[step], block), send_sem.at[step, block])


def local_kernel(leads, members, matrix_tiles, tile_slot, tile_cols, send_rows, residual, diag_inv):
    share_tiles, tile_size, _ = matrix_tiles.shape
    rows, width = residual.shape
    smem = pl.BlockSpec(memory_space=pltpu.SMEM)
    vmem = pl.BlockSpec(memory_space=pltpu.VMEM)
    anywhere = pl.BlockSpec(memory_space=pl.ANY)
    work = 3 * 2 * rows * share_tiles * members * tile_size * width
    return pl.pallas_call(
        functools.partial(smoother_kernel, leads, members),
        out_shape=jax.ShapeDtypeStruct(residual.shape, residual.dtype),
        in_specs=[smem, smem, anywhere, anywhere, anywhere],
        out_specs=vmem,
        scratch_shapes=[
            pltpu.VMEM((rows, width), residual.dtype),
            pltpu.VMEM((1, rows), diag_inv.dtype),
            pltpu.VMEM((members * share_tiles, rows, tile_size), jnp.bfloat16),
            *[pltpu.VMEM((3, tile_size, width), jnp.bfloat16)] * 3,
            pltpu.SemaphoreType.DMA((3,)),
            pltpu.SemaphoreType.DMA,
            pltpu.SemaphoreType.DMA,
            pltpu.SemaphoreType.DMA((3, 3)),
            pltpu.SemaphoreType.DMA((3, 3)),
            pltpu.SemaphoreType.DMA((3, members - 1)),
        ],
        cost_estimate=pl.CostEstimate(
            flops=work, bytes_accessed=matrix_tiles.size * 2 + residual.size * 8, transcendentals=0
        ),
        compiler_params=pltpu.CompilerParams(
            collective_id=0, has_side_effects=True, vmem_limit_bytes=60 * 1024 * 1024
        ),
    )(tile_slot, tile_cols, matrix_tiles, residual, diag_inv.reshape(1, rows))


def local(*args):
    leads, members = lax.axis_size("lead"), lax.axis_size("grp")
    if args[2].shape[0] == 1 and leads > 2 and leads % 2 == 0 and members > 1:
        return local_kernel(leads, members, *args)
    return local_general(*args)


def solution(mesh):
    in_specs = (
        P(("lead", "grp"), None, None),
        P("lead", None),
        P("lead", None),
        P(),
        P(("lead", "grp"), None),
        P(("lead", "grp")),
    )
    out_specs = P(("lead", "grp"), None)
    return jax.shard_map(local, mesh=mesh, in_specs=in_specs, out_specs=out_specs, check_vma=False)
```

```python
import functools

import jax
import jax.numpy as jnp
from jax import lax
from jax.experimental import pallas as pl
from jax.experimental.pallas import tpu as pltpu
from jax.sharding import PartitionSpec as P

TILES_ROW = 8


lower_bound = 0.5
upper_bound = 1.5


def from_behind(shard, axis, by):
    devices = lax.axis_size(axis)
    return lax.ppermute(shard, axis, [(i, (i + by) % devices) for i in range(devices)])


def one_sweep(start_residual, inverse, apply_operator):
    center_value = (upper_bound + lower_bound) / 2.0
    half_width = (upper_bound - lower_bound) / 2.0
    ratio_value = center_value / half_width
    update = inverse[:, None] * start_residual / center_value
    approx = update
    rho_now = 1.0 / ratio_value
    rho_next = 1.0 / (2.0 * ratio_value - rho_now)
    remaining = start_residual - apply_operator(approx)
    update = (
        rho_next * rho_now * update + 2.0 * rho_next / half_width * inverse[:, None] * remaining
    )
    approx = approx + update
    return approx


def smooth_twice(rhs_field, inverse, apply_operator):
    first_pass = one_sweep(rhs_field, inverse, apply_operator)
    remaining = rhs_field - apply_operator(first_pass)
    second_pass = one_sweep(remaining, inverse, apply_operator)
    return first_pass + second_pass


def pick_blocks(blocks, rows):
    return jnp.concatenate(
        [lax.dynamic_slice_in_dim(blocks, rows[i], 1, 0) for i in range(rows.shape[0])], axis=0
    )


def extend(blocks, send_rows):
    position = lax.axis_index("lead")
    mine_up = pick_blocks(blocks, send_rows[position, 0])
    mine_down = pick_blocks(blocks, send_rows[position, 1])
    from_lower = from_behind(mine_up, "lead", 1)
    from_upper = from_behind(mine_down, "lead", -1)
    return jnp.concatenate([blocks, from_lower, from_upper], axis=0)


def local_general(matrix_tiles, tile_slot, tile_cols, send_rows, residual, diag_inv):
    block_rows = tile_cols.shape[0]
    tile_size = matrix_tiles.shape[1]
    member = lax.axis_index("grp")
    share_rows = residual.shape[0]
    group_slots = tile_slot[0]
    share_tiles = matrix_tiles.shape[0]
    members = lax.axis_size("grp")
    own_slots = lax.dynamic_slice_in_dim(group_slots, member * share_tiles, share_tiles, 0)
    own_block = own_slots // TILES_ROW
    target = jnp.arange(members, dtype=jnp.int32)[:, None, None]
    offsets = jnp.arange(share_rows, dtype=jnp.int32)[None, None, :]
    source_row = target * share_rows + offsets - own_block[None, :, None] * tile_size
    valid = (source_row >= 0) & (source_row < tile_size)
    clipped = jnp.clip(source_row, 0, tile_size - 1)
    tile_pick = jnp.arange(share_tiles, dtype=jnp.int32)[None, :, None]
    picked = matrix_tiles[tile_pick, clipped]
    outgoing = jnp.where(valid[..., None], picked, jnp.zeros_like(picked))
    received = lax.all_to_all(outgoing, "grp", split_axis=0, concat_axis=0, tiled=True)
    flat_rows = received.reshape(members * share_tiles, share_rows * tile_size)
    position_of = group_slots % TILES_ROW
    selector = (jnp.arange(TILES_ROW, dtype=jnp.int32)[:, None] == position_of[None, :]).astype(
        jnp.bfloat16
    )
    mine = jnp.dot(selector, flat_rows, preferred_element_type=jnp.float32).astype(jnp.bfloat16)
    mine = mine.reshape(TILES_ROW, share_rows, tile_size).transpose(1, 0, 2)
    mine = mine.reshape(share_rows, TILES_ROW * tile_size)
    first_block = member * share_rows // tile_size
    row_block = (member * share_rows + jnp.arange(share_rows, dtype=jnp.int32)) // tile_size

    def apply_operator(approx):
        rounded = approx.astype(jnp.bfloat16)
        gathered = lax.all_gather(rounded, "grp", axis=0, tiled=True)
        extended = extend(gathered.reshape(block_rows, tile_size, -1), send_rows)
        target_block = jnp.minimum(first_block + 0, block_rows - 1)
        operand = pick_blocks(extended, tile_cols[target_block])
        operand = operand.reshape(TILES_ROW * tile_size, -1)
        product = jnp.dot(mine, operand, preferred_element_type=jnp.float32)
        coupled = jnp.where((row_block == first_block + 0)[:, None], product, 0.0)
        return approx / diag_inv[:, None] + coupled

    correction = smooth_twice(residual, diag_inv, apply_operator)
    return correction


MESH = pl.DeviceIdType.MESH


def smoother_kernel(
    leads, members, slot_ref, cols_ref, tiles_ref, rhs_in, inv_in, out_ref,
    rhs_ref, inv_ref, mine, ext0, ext1, ext2, local_sem, tile_send, tile_recv, send_sem, recv_sem, group_sem,
):
    lead, me = lax.axis_index("lead"), lax.axis_index("grp")
    exts = (ext0, ext1, ext2)
    share_tiles, tile_size, _ = tiles_ref.shape
    rows, width = rhs_in.shape
    total_tiles = share_tiles * members
    odd = lax.rem(lead, 2)
    mate = lead + 1 - 2 * odd
    far = lax.rem(lead + leads - 1 + 2 * odd, leads)
    at_mate, at_far = 1 + odd, 2 - odd
    others = [lax.rem(me + i, members) for i in range(1, members)]
    everyone = [me] + others

    partners = [(lead, p) for p in others]
    partners += [(far, p) for p in everyone] + [(mate, me)]
    barrier = pltpu.get_barrier_semaphore()
    for partner in partners:
        pl.semaphore_signal(barrier, inc=1, device_id=partner, device_id_type=MESH)

    def rows_of(member):
        return pl.ds(pl.multiple_of(member * rows, rows), rows)

    def pieces(ext, block):
        return ext.at[block] if block else ext.at[0, pl.ds(0, (members - 1) * rows)]

    landing = mine.at[pl.ds(me * share_tiles, share_tiles)]
    load_rhs = pltpu.make_async_copy(rhs_in, rhs_ref, local_sem.at[0])
    load_rhs.start()
    load_inv = pltpu.make_async_copy(inv_in, inv_ref, local_sem.at[1])
    load_inv.start()
    own_copy = pltpu.make_async_copy(tiles_ref.at[:, rows_of(me), :], landing, local_sem.at[2])
    own_copy.start()
    columns = [cols_ref[0, lax.rem(slot_ref[0, t], TILES_ROW)] for t in range(total_tiles)]

    load_rhs.wait()
    load_inv.wait()

    row_id = lax.broadcasted_iota(jnp.int32, (rows, rows), 0)
    col_id = lax.broadcasted_iota(jnp.int32, (rows, rows), 1)
    inverse = jnp.broadcast_to(inv_ref[...], (rows, rows))
    inverse = jnp.sum(jnp.where(row_id == col_id, inverse, 0.0), axis=1, keepdims=True)
    rhs = rhs_ref[...]

    def push(step, field):
        ext = exts[step]
        here = ext.at[0, rows_of(me), :]
        here[...] = field.astype(jnp.bfloat16)
        if step == 0:
            pl.semaphore_wait(barrier, len(partners))
        for i, p in enumerate(others):
            pltpu.make_async_remote_copy(
                src_ref=here, dst_ref=here,
                send_sem=send_sem.at[step, 0], recv_sem=group_sem.at[step, i],
                device_id=(lead, p), device_id_type=MESH,
            ).start()
        for p in everyone:
            pltpu.make_async_remote_copy(
                src_ref=here, dst_ref=ext.at[at_far, rows_of(me), :],
                send_sem=send_sem.at[step, 1], recv_sem=recv_sem.at[step, at_far],
                device_id=(far, p), device_id_type=MESH,
            ).start()
        pass_on(step, me)
        if step == 0:
            for p in others:
                pltpu.make_async_remote_copy(
                    src_ref=tiles_ref.at[:, rows_of(p), :], dst_ref=landing,
                    send_sem=tile_send, recv_sem=tile_recv,
                    device_id=(lead, p), device_id_type=MESH,
                ).start()

    def pass_on(step, owner):
        ext = exts[step]
        pltpu.make_async_remote_copy(
            src_ref=ext.at[0, rows_of(owner), :], dst_ref=ext.at[at_mate, rows_of(owner), :],
            send_sem=send_sem.at[step, 2], recv_sem=recv_sem.at[step, at_mate],
            device_id=(mate, me), device_id_type=MESH,
        ).start()

    def wait_for(ref, sem):
        pltpu.make_async_copy(ref, ref, sem).wait()

    def coupled(step):
        ext = exts[step]
        for i in range(1, members):
            owner = lax.rem(me + members - i, members)
            wait_for(ext.at[0, rows_of(owner), :], group_sem.at[step, i - 1])
            pass_on(step, owner)
        for block in (1, 2):
            wait_for(ext.at[block], recv_sem.at[step, block])
        if step == 0:
            own_copy.wait()
            wait_for(mine.at[pl.ds(0, (members - 1) * share_tiles)], tile_recv)
        left = jnp.concatenate([mine[t] for t in range(total_tiles)], axis=1)
        right = jnp.concatenate([ext[columns[t]] for t in range(total_tiles)], axis=0)
        return jnp.dot(left, right, preferred_element_type=jnp.float32)

    center = (upper_bound + lower_bound) / 2.0
    half = (upper_bound - lower_bound) / 2.0
    sigma = center / half
    rho = 1.0 / sigma
    rho_next = 1.0 / (2.0 * sigma - rho)
    keep, gain = 1.0 + rho_next * rho, 2.0 * rho_next / half
    rest = 1.0 - 1.0 / center

    def sweep(step, start):
        push(step, inverse * (start * (1.0 / center)))
        product = coupled(step)
        scaled = keep / center * start + gain * (rest * start - product)
        return inverse * scaled, scaled

    first, first_scaled = sweep(0, rhs)
    push(1, first)
    remaining = rhs - (first_scaled + coupled(1))
    second, _ = sweep(2, remaining)
    out_ref[...] = first + second

    wait_for(tiles_ref.at[:, pl.ds(0, (members - 1) * rows), :], tile_send)
    for step in range(3):
        for block in range(3):
            wait_for(pieces(exts[step], block), send_sem.at[step, block])


def local_kernel(leads, members, matrix_tiles, tile_slot, tile_cols, send_rows, residual, diag_inv):
    share_tiles, tile_size, _ = matrix_tiles.shape
    rows, width = residual.shape
    smem = pl.BlockSpec(memory_space=pltpu.SMEM)
    vmem = pl.BlockSpec(memory_space=pltpu.VMEM)
    anywhere = pl.BlockSpec(memory_space=pl.ANY)
    work = 3 * 2 * rows * share_tiles * members * tile_size * width
    return pl.pallas_call(
        functools.partial(smoother_kernel, leads, members),
        out_shape=jax.ShapeDtypeStruct(residual.shape, residual.dtype),
        in_specs=[smem, smem, anywhere, anywhere, anywhere],
        out_specs=vmem,
        scratch_shapes=[
            pltpu.VMEM((rows, width), residual.dtype),
            pltpu.VMEM((1, rows), diag_inv.dtype),
            pltpu.VMEM((members * share_tiles, rows, tile_size), jnp.bfloat16),
            *[pltpu.VMEM((3, tile_size, width), jnp.bfloat16)] * 3,
            pltpu.SemaphoreType.DMA((3,)),
            pltpu.SemaphoreType.DMA,
            pltpu.SemaphoreType.DMA,
            pltpu.SemaphoreType.DMA((3, 3)),
            pltpu.SemaphoreType.DMA((3, 3)),
            pltpu.SemaphoreType.DMA((3, members - 1)),
        ],
        cost_estimate=pl.CostEstimate(
            flops=work, bytes_accessed=matrix_tiles.size * 2 + residual.size * 8, transcendentals=0
        ),
        compiler_params=pltpu.CompilerParams(
            collective_id=0, has_side_effects=True, vmem_limit_bytes=55168 * 1024
        ),
    )(tile_slot, tile_cols, matrix_tiles, residual, diag_inv.reshape(1, rows))


def local(*args):
    leads, members = lax.axis_size("lead"), lax.axis_size("grp")
    if args[2].shape[0] == 1 and leads > 2 and leads % 2 == 0 and members > 1:
        return local_kernel(leads, members, *args)
    return local_general(*args)


def solution(mesh):
    in_specs = (
        P(("lead", "grp"), None, None),
        P("lead", None),
        P("lead", None),
        P(),
        P(("lead", "grp"), None),
        P(("lead", "grp")),
    )
    out_specs = P(("lead", "grp"), None)
    return jax.shard_map(local, mesh=mesh, in_specs=in_specs, out_specs=out_specs, check_vma=False)
```
